512 devices in a mesh: stretch: 16 (over z_hi, y, core), worker: 32 (over x, z_lo).
Axes of the slice: x: 4, y: 4, z: 16 (z_hi: 2, z_lo: 8; z = z_hi * 8 + z_lo), core: 2. Of those that a mesh axis runs over, the one named last changes fastest.
Arguments:
- theta: bfloat16 [16, 32, 3, 512, 512], P('stretch', None, None, 'worker'), may hold values from -6 to 6
- gates: float32 [16, 32, 3, 3], P('stretch'), may hold values from -3.5 to 3.5
- edge_weights: float32 [16, 32, 512], P('stretch', None, 'worker'), may hold values from 0.25 to 2
- sizes: int32 [16, 32], P('stretch'), may hold values from 64 to 512
- ranks: int32 [16, 32], P('stretch'), may hold values from 6 to 48
- order: int32 [16, 32], P('stretch'), may hold values from 0 to 31, each once within a row
- sketch: bfloat16 [16, 512, 48], P('stretch'), may hold values from -0.25 to 0.25
Outputs:
- factors: bfloat16 [16, 32, 48, 512], P('stretch', 'worker')
The draws below stay inside these ranges and needn't reach their ends.
Inputs may be any that keep to these rules, and one draw needn't show every extreme that they name: Each row order[s, :] is a permutation of 0 to 31.
All inputs are finite; a program needn't handle non-finite values.
Results may differ from the reference program's by a relative error of at most 0.0053.
Values may be sent and summed in bfloat16 or wider, within the bound.
No kernel may reach another device: no remote copies, remote signals or barrier semaphores. Data moves between devices by JAX's collectives and lax.ppermute only.
A program may use at most 64 MiB of HBM per device.

```python
import math
import jax
import jax.numpy as jnp
from jax import lax

BS = 512
K = 48
NBLK = 32
STRETCHES = 16


def touch_ends(array, own_key, least, high):
    dims = array.shape
    spot = [jax.random.randint(jax.random.fold_in(own_key, axis), (), 0, dims[axis]) for axis in range(len(dims))]
    array = array.at[tuple(spot)].set(least)
    longest = dims.index(max(dims))
    spot[longest] = (spot[longest] + 1) % dims[longest]
    return array.at[tuple(spot)].set(high)


def steps_of(rng, dims, cuts, smallest, high):
    gain = 1.0
    for position, parts in cuts:
        heights = jax.random.uniform(jax.random.fold_in(jax.random.fold_in(rng, 6), position), (parts,), jnp.float32, smallest / len(cuts), high / len(cuts))
        gain = gain * jnp.repeat(jnp.exp(heights), dims[position] // parts).reshape((-1,) + (1,) * (len(dims) - 1 - position))
    return gain


def gaussian(key, dims, width, most, pieces=(), kind=jnp.bfloat16):
    values = width * jax.random.normal(key, dims, jnp.float32)
    if pieces:
        values = values * steps_of(key, dims, pieces, -0.22, 0.18)
    return jnp.clip(values, -most, most).astype(kind)


def setup_inputs(seed: int = 0) -> dict:
    key_list = jax.random.split(jax.random.key(seed), 8)
    theta = gaussian(key_list[0], (STRETCHES, NBLK, 3, BS, BS), 1.0, 6.0, ((0, 16), (3, 32)))
    gates = gaussian(key_list[1], (STRETCHES, NBLK, 3, 3), 3 ** -0.5, 3.5, ((0, 16),), jnp.float32)
    edge_weights = jnp.clip(jnp.exp(math.log(2.0) - 2.0794415 * jax.random.uniform(key_list[2], (STRETCHES, NBLK, BS), jnp.float32) ** steps_of(key_list[2], (STRETCHES, NBLK, BS), ((0, 16), (2, 32)), -0.2, 0.2)), 0.25, 2.0)
    sizes = touch_ends(jax.random.randint(key_list[3], (STRETCHES, NBLK), BS // 8, BS + 1), jax.random.fold_in(key_list[3], 1), BS // 8, BS).astype(jnp.int32)
    ranks = touch_ends(jax.random.randint(key_list[4], (STRETCHES, NBLK), K // 8, K + 1), jax.random.fold_in(key_list[4], 1), K // 8, K).astype(jnp.int32)
    order = jax.vmap(lambda own: jax.random.permutation(own, NBLK))(jax.random.split(key_list[5], STRETCHES)).reshape((STRETCHES, NBLK)).astype(jnp.int32)
    sketch = gaussian(key_list[6], (STRETCHES, BS, K), BS ** -0.5, 0.25, ((0, 16),))
    return dict(theta=theta, gates=gates, edge_weights=edge_weights, sizes=sizes, ranks=ranks, order=order, sketch=sketch)


def factor_block(args):
    theta, gates, weights, size, rank, sketch = args
    mixed = jnp.einsum('gp,pab->gab', gates, theta.astype(jnp.float32), precision=lax.Precision.HIGHEST)
    index = jnp.arange(BS, dtype=jnp.int32)
    live = (index < size).astype(jnp.float32)
    mixed = mixed * live[None, :, None] * live[None, None, :]
    mixed = mixed * weights[None, :, None]
    block = mixed.reshape(3 * BS, BS).astype(jnp.bfloat16)
    kept = jnp.minimum(rank, size // 2)
    columns = (jnp.arange(K, dtype=jnp.int32) < kept).astype(jnp.float32)
    sample = jnp.dot(block.astype(jnp.float32), sketch.astype(jnp.float32), preferred_element_type=jnp.float32)
    sample = (sample * columns[None, :]).astype(jnp.bfloat16)
    gram = jnp.dot(sample.T.astype(jnp.float32), sample.astype(jnp.float32), preferred_element_type=jnp.float32)
    gram = gram + (1.0 - columns)[:, None] * jnp.eye(K, dtype=jnp.float32)
    projected = jnp.dot(sample.T.astype(jnp.float32), block.astype(jnp.float32), preferred_element_type=jnp.float32)
    lower = jnp.linalg.cholesky(gram)
    return jax.scipy.linalg.solve_triangular(lower, projected, lower=True)

def one_stretch(args):
    theta, gates, weights, sizes, ranks, order, sketch = args
    count = order.shape[0]
    right = lax.map(lambda one: factor_block(one + (sketch,)), (theta[order], gates[order], weights[order], sizes[order], ranks[order]))
    total = jnp.sum(right * right)
    scale = jnp.sqrt(jnp.float32(count) / total)
    return (right * scale).astype(jnp.bfloat16)

def reference(theta, gates, edge_weights, sizes, ranks, order, sketch):
    left_weights = jnp.roll(edge_weights, 1, axis=0)
    return lax.map(one_stretch, (theta, gates, left_weights, sizes, ranks, order, sketch))
```

```python
import functools

import jax
import jax.numpy as jnp
from jax import lax
from jax.experimental import pallas as pl
from jax.experimental.pallas import tpu as pltpu
from jax.sharding import PartitionSpec as P

NX = 4
NZ = 8
PAIRS = NZ // 2
NEAR = NX * 2
WORKERS = NX * NZ
NEAR_GROUPS = [[x * NZ + 2 * p + q for x in range(NX) for q in range(2)] for p in range(PAIRS)]
FAR_GROUPS = [[x * NZ + 2 * p + q for p in range(PAIRS)] for x in range(NX) for q in range(2)]
GRAM_LANES = 128
LOW_LANE = 64


def place():
    me = lax.axis_index("worker")
    column, depth = me // NZ, me % NZ
    return me, column, depth // 2, depth % 2


def arrange_kernel(order, theta, message):
    for d in range(NEAR):
        for j in range(PAIRS):
            owner = (d // 2) * NZ + 2 * j + d % 2
            message[d, j] = theta[order[owner]]


def contract_kernel(order, sizes, gates, rows_in, weights, sketch, out, block):
    _, column, pair, parity = place()
    near, _, _, depth, width = rows_in.shape
    rank = sketch.shape[1]
    total = near * depth
    lane = lax.broadcasted_iota(jnp.int32, (depth, weights.shape[2]), 1)
    sub = lax.broadcasted_iota(jnp.int32, (depth, 1), 0)
    bond = lax.broadcasted_iota(jnp.int32, (width, rank), 0)
    for j in range(PAIRS):
        blk = order[column * NZ + 2 * j + parity]
        size = sizes[blk]
        mix = [[gates[blk * 9 + g * 3 + p] for p in range(3)] for g in range(3)]
        for s in range(near):
            first = ((s // 2) * NZ + 2 * pair + s % 2) * depth
            scale = jnp.sum(jnp.where(lane == blk, weights[s], 0.0), axis=1, keepdims=True)
            scale = jnp.where(sub + first < size, scale, 0.0)
            x0, x1, x2 = (rows_in[s, j, p].astype(jnp.float32) for p in range(3))
            for g in range(3):
                mixed = (mix[g][0] * x0 + mix[g][1] * x1 + mix[g][2] * x2) * scale
                at = g * total + s * depth
                block[at : at + depth, :] = mixed.astype(jnp.bfloat16)
        live = jnp.where(bond < size, sketch[...].astype(jnp.float32), 0.0).astype(jnp.bfloat16)
        rows = block[...]
        sample = jnp.dot(rows, live, preferred_element_type=jnp.float32).astype(jnp.bfloat16)
        over_rows = (((0,), (0,)), ((), ()))
        projected = lax.dot_general(sample, rows, over_rows, preferred_element_type=jnp.float32)
        gram = lax.dot_general(sample, sample, over_rows, preferred_element_type=jnp.float32)
        high = gram.astype(jnp.bfloat16)
        low = (gram - high.astype(jnp.float32)).astype(jnp.bfloat16)
        out[j, :, :width] = projected.astype(jnp.bfloat16)
        out[j, :, width : width + rank] = high
        out[j, :, width + LOW_LANE : width + LOW_LANE + rank] = low


def solve_kernel(order, sizes, ranks, parts, right_out, norm_out, wide):
    me = place()[0]
    pairs, rank, full = parts.shape
    width = full - GRAM_LANES
    blk = order[me]
    size = sizes[blk]
    kept = jnp.minimum(ranks[blk], size // 2)

    tail = parts[0, :, width:].astype(jnp.float32)
    for p in range(1, pairs):
        tail = tail + parts[p, :, width:].astype(jnp.float32)
    row = lax.broadcasted_iota(jnp.int32, (rank, GRAM_LANES), 0)
    lane = lax.broadcasted_iota(jnp.int32, (rank, GRAM_LANES), 1)
    gram = tail + pltpu.roll(tail, GRAM_LANES - LOW_LANE, 1)
    gram = jnp.where((row < kept) & (lane < kept), gram, 0.0)
    gram = jnp.where((row == lane) & (row >= kept), 1.0, gram)
    work = jnp.where(lane == row + LOW_LANE, 1.0, gram)

    step = 8
    inverse = []
    for k0 in range(0, rank, step):
        height = rank - k0
        heads = [work[j : j + 1, :] for j in range(step)]
        cols = [
            jnp.broadcast_to(work[:, k0 + j : k0 + j + 1], (height, GRAM_LANES))
            for j in range(step)
        ]
        scaled = []
        for j in range(step):
            pivot = cols[j][j : j + 1, :]
            inv = 1.0 / pivot
            scaled.append(heads[j] * inv)
            inverse.append(heads[j] * lax.rsqrt(pivot))
            for i in range(j + 1, step):
                factor = cols[j][i : i + 1, :]
                heads[i] = heads[i] - factor * scaled[j]
                cols[i] = cols[i] - cols[j] * (factor * inv)
        if height > step:
            work = work[step:, :]
            for j in range(step):
                work = work - cols[j][step:, :] * scaled[j]
    lower_inverse = jnp.concatenate(inverse, axis=0)
    lower_inverse = jnp.where(lane >= LOW_LANE, lower_inverse, 0.0)

    projected = parts[0, :, :width].astype(jnp.float32)
    for p in range(1, pairs):
        projected = projected + parts[p, :, :width].astype(jnp.float32)
    prow = lax.broadcasted_iota(jnp.int32, (rank, width), 0)
    plane = lax.broadcasted_iota(jnp.int32, (rank, width), 1)
    wide[...] = jnp.zeros_like(wide)
    wide[LOW_LANE : LOW_LANE + rank, :] = jnp.where((prow < kept) & (plane < size), projected, 0.0)
    right = jnp.dot(
        lower_inverse,
        wide[...],
        preferred_element_type=jnp.float32,
        precision=lax.Precision.HIGHEST,
    )
    right_out[...] = right
    square = right * right
    folded = square[:, 0:128]
    for c in range(128, width, 128):
        folded = folded + square[:, c : c + 128]
    folded = jnp.sum(folded, axis=0, keepdims=True)
    norm_out[...] = jnp.broadcast_to(folded, norm_out.shape)


def finish_kernel(count, right, norms, out):
    total = jnp.sum(jnp.sum(norms[...], axis=0, keepdims=True), axis=1, keepdims=True)
    out[...] = (right[...] * jnp.sqrt(count / total)).astype(out.dtype)


SMEM = pl.BlockSpec(memory_space=pltpu.SMEM)
VMEM = pl.BlockSpec(memory_space=pltpu.VMEM)


def body(theta, gates, edge_weights, sizes, ranks, order, sketch):
    theta, gates, edge_weights, sketch = theta[0], gates[0], edge_weights[0], sketch[0]
    sizes, ranks, order = sizes[0], ranks[0], order[0]
    count, phys, depth, width = theta.shape
    rank = sketch.shape[1]
    stretches = lax.axis_size("stretch")
    left = lax.ppermute(
        edge_weights, "stretch", [(i, (i + 1) % stretches) for i in range(stretches)]
    )
    message = pl.pallas_call(
        arrange_kernel,
        out_shape=jax.ShapeDtypeStruct((NEAR, PAIRS, phys, depth, width), theta.dtype),
        in_specs=[SMEM, VMEM],
        out_specs=VMEM,
        name="arrange",
    )(order, theta)
    rows_in = lax.all_to_all(
        message, "worker", 0, 0, tiled=True, axis_index_groups=NEAR_GROUPS
    )
    weights = lax.all_to_all(
        jnp.broadcast_to(left.T[None], (NEAR, depth, count)),
        "worker",
        0,
        0,
        tiled=True,
        axis_index_groups=NEAR_GROUPS,
    )
    parts = pl.pallas_call(
        contract_kernel,
        out_shape=jax.ShapeDtypeStruct((PAIRS, rank, width + GRAM_LANES), jnp.bfloat16),
        in_specs=[SMEM, SMEM, SMEM, VMEM, VMEM, VMEM],
        out_specs=VMEM,
        scratch_shapes=[pltpu.VMEM((3 * NEAR * depth, width), jnp.bfloat16)],
        compiler_params=pltpu.CompilerParams(vmem_limit_bytes=32 * 2**20),
        name="contract",
    )(order, sizes, gates.reshape(-1), rows_in, weights, sketch)
    parts = lax.all_to_all(parts, "worker", 0, 0, tiled=True, axis_index_groups=FAR_GROUPS)
    right, norms = pl.pallas_call(
        solve_kernel,
        out_shape=(
            jax.ShapeDtypeStruct((rank, width), jnp.float32),
            jax.ShapeDtypeStruct((WORKERS, 128), jnp.float32),
        ),
        in_specs=[SMEM, SMEM, SMEM, VMEM],
        out_specs=(VMEM, VMEM),
        scratch_shapes=[pltpu.VMEM((GRAM_LANES, width), jnp.float32)],
        name="solve",
    )(order, sizes, ranks, parts)
    norms = lax.all_to_all(norms, "worker", 0, 0, tiled=True)
    factors = pl.pallas_call(
        functools.partial(finish_kernel, float(count)),
        out_shape=jax.ShapeDtypeStruct((rank, width), jnp.bfloat16),
        in_specs=[VMEM, VMEM],
        out_specs=VMEM,
        name="finish",
    )(right, norms)
    return factors[None, None]


def solution(mesh):
    return jax.shard_map(
        body,
        mesh=mesh,
        in_specs=(
            P("stretch", None, None, "worker", None),
            P("stretch", None, None, None),
            P("stretch", None, "worker"),
            P("stretch", None),
            P("stretch", None),
            P("stretch", None),
            P("stretch", None, None),
        ),
        out_specs=P("stretch", "worker", None, None),
        check_vma=False,
    )
```

```python
import functools

import jax
import jax.numpy as jnp
from jax import lax
from jax.experimental import pallas as pl
from jax.experimental.pallas import tpu as pltpu
from jax.sharding import PartitionSpec as P

NX = 4
NZ = 8
PAIRS = NZ // 2
NEAR = NX * 2
WORKERS = NX * NZ
NEAR_GROUPS = [[x * NZ + 2 * p + q for x in range(NX) for q in range(2)] for p in range(PAIRS)]
FAR_GROUPS = [[x * NZ + 2 * p + q for p in range(PAIRS)] for x in range(NX) for q in range(2)]
GRAM_LANES = 128
LOW_LANE = 64


def place():
    me = lax.axis_index("worker")
    column, depth = me // NZ, me % NZ
    return me, column, depth // 2, depth % 2


def mix_kernel(gates, theta, mixed):
    for blk in range(theta.shape[0]):
        x = [theta[blk, p].astype(jnp.float32) for p in range(3)]
        for g in range(3):
            mixed[blk, g] = (
                gates[g, 0, blk] * x[0] + gates[g, 1, blk] * x[1] + gates[g, 2, blk] * x[2]
            )


def weigh_kernel(order, sizes, mixed, left, message):
    depth, width = mixed.shape[2:]
    first = place()[0] * depth
    columns = left[...]
    lane = lax.broadcasted_iota(jnp.int32, columns.shape, 1)
    row = lax.broadcasted_iota(jnp.int32, (depth, 1), 0) + first
    bond = lax.broadcasted_iota(jnp.int32, (1, width), 1)
    for d in range(NEAR):
        for j in range(PAIRS):
            blk = order[(d // 2) * NZ + 2 * j + d % 2]
            size = sizes[blk]
            scale = jnp.sum(jnp.where(lane == blk, columns, 0.0), axis=1, keepdims=True)
            scale = jnp.where(row < size, scale, 0.0)
            for g in range(3):
                rows = jnp.where(bond < size, mixed[blk, g] * scale, 0.0)
                message[d, j, g] = rows.astype(jnp.bfloat16)


def contract_kernel(rows_in, sketch, out):
    near, pairs, phys, depth, width = rows_in.shape
    rank = sketch.shape[0]
    basis = sketch[...]
    over_bond = (((1,), (1,)), ((), ()))
    over_rows = (((0,), (0,)), ((), ()))
    for j in range(pairs):
        rows = rows_in[:, j].reshape(near * phys * depth, width)
        sample = lax.dot_general(rows, basis, over_bond, preferred_element_type=jnp.float32)
        sample = sample.astype(jnp.bfloat16)
        projected = lax.dot_general(sample, rows, over_rows, preferred_element_type=jnp.float32)
        gram = lax.dot_general(sample, sample, over_rows, preferred_element_type=jnp.float32)
        high = gram.astype(jnp.bfloat16)
        low = (gram - high.astype(jnp.float32)).astype(jnp.bfloat16)
        out[j, :, :width] = projected.astype(jnp.bfloat16)
        out[j, :, width : width + rank] = high
        out[j, :, width + LOW_LANE : width + LOW_LANE + rank] = low


def solve_kernel(order, sizes, ranks, parts, right_out, norm_out, wide):
    me = place()[0]
    pairs, rank, full = parts.shape
    width = full - GRAM_LANES
    blk = order[me]
    size = sizes[blk]
    kept = jnp.minimum(ranks[blk], size // 2)

    tail = parts[0, :, width:].astype(jnp.float32)
    for p in range(1, pairs):
        tail = tail + parts[p, :, width:].astype(jnp.float32)
    row = lax.broadcasted_iota(jnp.int32, (rank, GRAM_LANES), 0)
    lane = lax.broadcasted_iota(jnp.int32, (rank, GRAM_LANES), 1)
    gram = tail + pltpu.roll(tail, GRAM_LANES - LOW_LANE, 1)
    gram = jnp.where((row < kept) & (lane < kept), gram, 0.0)
    gram = jnp.where((row == lane) & (row >= kept), 1.0, gram)
    work = jnp.where(lane == row + LOW_LANE, 1.0, gram)

    step = 8
    inverse = []
    for k0 in range(0, rank, step):
        height = rank - k0
        heads = [work[j : j + 1, :] for j in range(step)]
        cols = [
            jnp.broadcast_to(work[:, k0 + j : k0 + j + 1], (height, GRAM_LANES))
            for j in range(step)
        ]
        scaled = []
        for j in range(step):
            pivot = cols[j][j : j + 1, :]
            inv = 1.0 / pivot
            scaled.append(heads[j] * inv)
            inverse.append(heads[j] * lax.rsqrt(pivot))
            for i in range(j + 1, step):
                factor = cols[j][i : i + 1, :]
                heads[i] = heads[i] - factor * scaled[j]
                cols[i] = cols[i] - cols[j] * (factor * inv)
        if height > step:
            work = work[step:, :]
            for j in range(step):
                work = work - cols[j][step:, :] * scaled[j]
    lower_inverse = jnp.concatenate(inverse, axis=0)
    lower_inverse = jnp.where(lane >= LOW_LANE, lower_inverse, 0.0)

    projected = parts[0, :, :width].astype(jnp.float32)
    for p in range(1, pairs):
        projected = projected + parts[p, :, :width].astype(jnp.float32)
    prow = lax.broadcasted_iota(jnp.int32, (rank, width), 0)
    wide[...] = jnp.zeros_like(wide)
    wide[LOW_LANE : LOW_LANE + rank, :] = jnp.where(prow < kept, projected, 0.0)
    right = jnp.dot(
        lower_inverse,
        wide[...],
        preferred_element_type=jnp.float32,
        precision=lax.Precision.HIGHEST,
    )
    right_out[...] = right
    square = right * right
    folded = square[:, 0:128]
    for c in range(128, width, 128):
        folded = folded + square[:, c : c + 128]
    folded = jnp.sum(folded, axis=0, keepdims=True)
    norm_out[...] = jnp.broadcast_to(folded, norm_out.shape)


def finish_kernel(count, right, norms, out):
    total = jnp.sum(jnp.sum(norms[...], axis=0, keepdims=True), axis=1, keepdims=True)
    out[...] = (right[...] * jnp.sqrt(count / total)).astype(out.dtype)


SMEM = pl.BlockSpec(memory_space=pltpu.SMEM)
VMEM = pl.BlockSpec(memory_space=pltpu.VMEM)


def body(theta, gates, edge_weights, sizes, ranks, order, sketch):
    theta, gates, edge_weights, sketch = theta[0], gates[0], edge_weights[0], sketch[0]
    sizes, ranks, order = sizes[0], ranks[0], order[0]
    count, phys, depth, width = theta.shape
    rank = sketch.shape[1]
    stretches = lax.axis_size("stretch")
    left = lax.ppermute(
        edge_weights.T, "stretch", [(i, (i + 1) % stretches) for i in range(stretches)]
    )
    mixed = pl.pallas_call(
        mix_kernel,
        out_shape=jax.ShapeDtypeStruct(theta.shape, jnp.float32),
        in_specs=[SMEM, VMEM],
        out_specs=VMEM,
        compiler_params=pltpu.CompilerParams(vmem_limit_bytes=16 * 2**20),
        cost_estimate=pl.CostEstimate(
            flops=15 * theta.size, bytes_accessed=6 * theta.size, transcendentals=0
        ),
        name="mix",
    )(jnp.transpose(gates, (1, 2, 0)), theta)
    message = pl.pallas_call(
        weigh_kernel,
        out_shape=jax.ShapeDtypeStruct((NEAR, PAIRS, phys, depth, width), theta.dtype),
        in_specs=[SMEM, SMEM, VMEM, VMEM],
        out_specs=VMEM,
        compiler_params=pltpu.CompilerParams(vmem_limit_bytes=16 * 2**20),
        name="weigh",
    )(order, sizes, mixed, left)
    rows_in = lax.all_to_all(
        message, "worker", 0, 0, tiled=True, axis_index_groups=NEAR_GROUPS
    )
    parts = pl.pallas_call(
        contract_kernel,
        out_shape=jax.ShapeDtypeStruct((PAIRS, rank, width + GRAM_LANES), jnp.bfloat16),
        in_specs=[VMEM, VMEM],
        out_specs=VMEM,
        compiler_params=pltpu.CompilerParams(vmem_limit_bytes=16 * 2**20),
        name="contract",
    )(rows_in, sketch.T)
    parts = lax.all_to_all(parts, "worker", 0, 0, tiled=True, axis_index_groups=FAR_GROUPS)
    right, norms = pl.pallas_call(
        solve_kernel,
        out_shape=(
            jax.ShapeDtypeStruct((rank, width), jnp.float32),
            jax.ShapeDtypeStruct((WORKERS, 128), jnp.float32),
        ),
        in_specs=[SMEM, SMEM, SMEM, VMEM],
        out_specs=(VMEM, VMEM),
        scratch_shapes=[pltpu.VMEM((GRAM_LANES, width), jnp.float32)],
        compiler_params=pltpu.CompilerParams(vmem_limit_bytes=16 * 2**20),
        name="solve",
    )(order, sizes, ranks, parts)
    norms = lax.all_to_all(norms, "worker", 0, 0, tiled=True)
    factors = pl.pallas_call(
        functools.partial(finish_kernel, float(count)),
        out_shape=jax.ShapeDtypeStruct((rank, width), jnp.bfloat16),
        in_specs=[VMEM, VMEM],
        out_specs=VMEM,
        compiler_params=pltpu.CompilerParams(vmem_limit_bytes=16 * 2**20),
        name="finish",
    )(right, norms)
    return factors[None, None]


def solution(mesh):
    return jax.shard_map(
        body,
        mesh=mesh,
        in_specs=(
            P("stretch", None, None, "worker", None),
            P("stretch", None, None, None),
            P("stretch", None, "worker"),
            P("stretch", None),
            P("stretch", None),
            P("stretch", None),
            P("stretch", None, None),
        ),
        out_specs=P("stretch", "worker", None, None),
        check_vma=False,
    )
```

```python
import functools

import jax
import jax.numpy as jnp
from jax import lax
from jax.experimental import pallas as pl
from jax.experimental.pallas import tpu as pltpu
from jax.sharding import PartitionSpec as P

NX = 4
NZ = 8
PAIRS = NZ // 2
NEAR = NX * 2
WORKERS = NX * NZ
NEAR_GROUPS = [[x * NZ + 2 * p + q for x in range(NX) for q in range(2)] for p in range(PAIRS)]
FAR_GROUPS = [[x * NZ + 2 * p + q for p in range(PAIRS)] for x in range(NX) for q in range(2)]
GRAM_LANES = 128
LOW_LANE = 64


def place():
    me = lax.axis_index("worker")
    column, depth = me // NZ, me % NZ
    return me, column, depth // 2, depth % 2


def mix_kernel(gates, theta, mixed):
    for blk in range(theta.shape[0]):
        x = [theta[blk, p].astype(jnp.float32) for p in range(3)]
        for g in range(3):
            mixed[blk, g] = (
                gates[g, 0, 0, blk] * x[0]
                + gates[g, 1, 0, blk] * x[1]
                + gates[g, 2, 0, blk] * x[2]
            )


def weigh_kernel(order, sizes, mixed, left, message):
    depth, width = mixed.shape[2:]
    first = place()[0] * depth
    columns = left[...]
    lane = lax.broadcasted_iota(jnp.int32, columns.shape, 1)
    row = lax.broadcasted_iota(jnp.int32, (depth, 1), 0) + first
    bond = lax.broadcasted_iota(jnp.int32, (1, width), 1)
    for d in range(NEAR):
        for j in range(PAIRS):
            blk = order[(d // 2) * NZ + 2 * j + d % 2]
            size = sizes[blk]
            scale = jnp.sum(jnp.where(lane == blk, columns, 0.0), axis=1, keepdims=True)
            scale = jnp.where(row < size, scale, 0.0)
            for g in range(3):
                rows = jnp.where(bond < size, mixed[blk, g] * scale, 0.0)
                message[d, j, g] = rows.astype(jnp.bfloat16)


def contract_kernel(rows_in, sketch, out, own):
    near, pairs, phys, depth, width = rows_in.shape
    rank = sketch.shape[0]
    pair = place()[2]
    basis = sketch[...]
    over_lanes = (((1,), (1,)), ((), ()))

    def rows_of(j):
        return rows_in[:, j].reshape(near * phys * depth, width)

    samples = []
    for j in range(pairs):
        sample = lax.dot_general(
            basis, rows_of(j), over_lanes, preferred_element_type=jnp.float32
        )
        samples.append(sample.astype(jnp.bfloat16))
    for j in range(pairs):
        sample = samples[j]
        projected = jnp.dot(sample, rows_of(j), preferred_element_type=jnp.float32)
        out[j] = projected.astype(jnp.bfloat16)

        @pl.when(pair == j)
        def _():
            own[...] = projected


def solve_kernel(order, sizes, ranks, parts, own, sketch, right_out, norm_out, wide):
    me, _, pair, _ = place()
    pairs, rank, width = parts.shape
    blk = order[me]
    size = sizes[blk]
    kept = jnp.minimum(ranks[blk], size // 2)

    projected = own[...]
    for p in range(pairs):
        projected = projected + jnp.where(pair == p, 0.0, parts[p].astype(jnp.float32))
    prow = lax.broadcasted_iota(jnp.int32, (rank, width), 0)
    projected = jnp.where(prow < kept, projected, 0.0)
    basis = jnp.concatenate(
        [sketch[...].astype(jnp.float32), jnp.zeros((GRAM_LANES - rank, width), jnp.float32)], axis=0
    )
    over_lanes = (((1,), (1,)), ((), ()))
    gram = lax.dot_general(
        projected,
        basis,
        over_lanes,
        preferred_element_type=jnp.float32,
        precision=lax.Precision.HIGHEST,
    )
    mirror = lax.dot_general(
        basis[:rank],
        jnp.concatenate([projected, jnp.zeros((GRAM_LANES - rank, width), jnp.float32)], axis=0),
        over_lanes,
        preferred_element_type=jnp.float32,
        precision=lax.Precision.HIGHEST,
    )
    row = lax.broadcasted_iota(jnp.int32, (rank, GRAM_LANES), 0)
    lane = lax.broadcasted_iota(jnp.int32, (rank, GRAM_LANES), 1)
    gram = jnp.where((row < kept) & (lane < kept), 0.5 * (gram + mirror), 0.0)
    gram = jnp.where((row == lane) & (row >= kept), 1.0, gram)
    work = jnp.where(lane == row + LOW_LANE, 1.0, gram)

    step = 8
    inverse = []
    for k0 in range(0, rank, step):
        height = rank - k0
        heads = [work[j : j + 1, :] for j in range(step)]
        cols = [
            jnp.broadcast_to(work[:, k0 + j : k0 + j + 1], (height, GRAM_LANES))
            for j in range(step)
        ]
        scaled = []
        for j in range(step):
            pivot = cols[j][j : j + 1, :]
            inv = 1.0 / pivot
            scaled.append(heads[j] * inv)
            inverse.append(heads[j] * lax.rsqrt(pivot))
            for i in range(j + 1, step):
                factor = cols[j][i : i + 1, :]
                heads[i] = heads[i] - factor * scaled[j]
                cols[i] = cols[i] - cols[j] * (factor * inv)
        if height > step:
            work = work[step:, :]
            for j in range(step):
                work = work - cols[j][step:, :] * scaled[j]
    lower_inverse = jnp.concatenate(inverse, axis=0)
    lower_inverse = jnp.where(lane >= LOW_LANE, lower_inverse, 0.0)

    wide[...] = jnp.zeros_like(wide)
    wide[LOW_LANE : LOW_LANE + rank, :] = projected
    right = jnp.dot(
        lower_inverse,
        wide[...],
        preferred_element_type=jnp.float32,
        precision=lax.Precision.HIGHEST,
    )
    right_out[...] = right
    square = right * right
    folded = square[:, 0:128]
    for c in range(128, width, 128):
        folded = folded + square[:, c : c + 128]
    folded = jnp.sum(folded, axis=0, keepdims=True)
    norm_out[...] = jnp.broadcast_to(folded, norm_out.shape)


def finish_kernel(count, right, norms, out):
    total = jnp.sum(jnp.sum(norms[...], axis=0, keepdims=True), axis=1, keepdims=True)
    out[...] = (right[...] * jnp.sqrt(count / total)).astype(out.dtype)


SMEM = pl.BlockSpec(memory_space=pltpu.SMEM)
VMEM = pl.BlockSpec(memory_space=pltpu.VMEM)


def body(theta, gates, edge_weights, sizes, ranks, order, sketch):
    theta, gates, edge_weights, sketch = theta[0], gates[0], edge_weights[0], sketch[0]
    sizes, ranks, order = sizes[0], ranks[0], order[0]
    count, phys, depth, width = theta.shape
    rank = sketch.shape[1]
    stretches = lax.axis_size("stretch")
    left = lax.ppermute(
        edge_weights.T, "stretch", [(i, (i + 1) % stretches) for i in range(stretches)]
    )
    mixed = pl.pallas_call(
        mix_kernel,
        out_shape=jax.ShapeDtypeStruct(theta.shape, jnp.float32),
        in_specs=[SMEM, VMEM],
        out_specs=VMEM,
        compiler_params=pltpu.CompilerParams(vmem_limit_bytes=16 * 2**20),
        cost_estimate=pl.CostEstimate(
            flops=15 * theta.size, bytes_accessed=6 * theta.size, transcendentals=0
        ),
        name="mix",
    )(jnp.transpose(gates, (1, 2, 0))[:, :, None], theta)
    message = pl.pallas_call(
        weigh_kernel,
        out_shape=jax.ShapeDtypeStruct((NEAR, PAIRS, phys, depth, width), theta.dtype),
        in_specs=[SMEM, SMEM, VMEM, VMEM],
        out_specs=VMEM,
        compiler_params=pltpu.CompilerParams(vmem_limit_bytes=16 * 2**20),
        name="weigh",
    )(order, sizes, mixed, left)
    rows_in = lax.all_to_all(
        message, "worker", 0, 0, tiled=True, axis_index_groups=NEAR_GROUPS
    )
    parts, own = pl.pallas_call(
        contract_kernel,
        out_shape=(
            jax.ShapeDtypeStruct((PAIRS, rank, width), jnp.bfloat16),
            jax.ShapeDtypeStruct((rank, width), jnp.float32),
        ),
        in_specs=[VMEM, VMEM],
        out_specs=(VMEM, VMEM),
        compiler_params=pltpu.CompilerParams(vmem_limit_bytes=16 * 2**20),
        name="contract",
    )(rows_in, sketch.T)
    parts = lax.all_to_all(parts, "worker", 0, 0, tiled=True, axis_index_groups=FAR_GROUPS)
    right, norms = pl.pallas_call(
        solve_kernel,
        out_shape=(
            jax.ShapeDtypeStruct((rank, width), jnp.float32),
            jax.ShapeDtypeStruct((WORKERS, 128), jnp.float32),
        ),
        in_specs=[SMEM, SMEM, SMEM, VMEM, VMEM, VMEM],
        out_specs=(VMEM, VMEM),
        scratch_shapes=[pltpu.VMEM((GRAM_LANES, width), jnp.float32)],
        compiler_params=pltpu.CompilerParams(vmem_limit_bytes=16 * 2**20),
        name="solve",
    )(order, sizes, ranks, parts, own, sketch.T)
    norms = lax.all_to_all(norms, "worker", 0, 0, tiled=True)
    factors = pl.pallas_call(
        functools.partial(finish_kernel, float(count)),
        out_shape=jax.ShapeDtypeStruct((rank, width), jnp.bfloat16),
        in_specs=[VMEM, VMEM],
        out_specs=VMEM,
        compiler_params=pltpu.CompilerParams(vmem_limit_bytes=16 * 2**20),
        name="finish",
    )(right, norms)
    return factors[None, None]


def solution(mesh):
    return jax.shard_map(
        body,
        mesh=mesh,
        in_specs=(
            P("stretch", None, None, "worker", None),
            P("stretch", None, None, None),
            P("stretch", None, "worker"),
            P("stretch", None),
            P("stretch", None),
            P("stretch", None),
            P("stretch", None, None),
        ),
        out_specs=P("stretch", "worker", None, None),
        check_vma=False,
    )
```

```python
import functools

import jax
import jax.numpy as jnp
from jax import lax
from jax.experimental import pallas as pl
from jax.experimental.pallas import tpu as pltpu
from jax.sharding import PartitionSpec as P

NX = 4
NZ = 8
PAIRS = NZ // 2
NEAR = NX * 2
WORKERS = NX * NZ
NEAR_GROUPS = [[x * NZ + 2 * p + q for x in range(NX) for q in range(2)] for p in range(PAIRS)]
FAR_GROUPS = [[x * NZ + 2 * p + q for p in range(PAIRS)] for x in range(NX) for q in range(2)]
LANES = 128
HALF = 64
OVER_LANES = (((1,), (1,)), ((), ()))


def place():
    me = lax.axis_index("worker")
    column, depth = me // NZ, me % NZ
    return me, column, depth // 2, depth % 2


def mix_kernel(gates, theta, mixed):
    for blk in range(theta.shape[0]):
        x = [theta[blk, p].astype(jnp.float32) for p in range(3)]
        for g in range(3):
            mixed[blk, g] = (
                gates[g, 0, 0, blk] * x[0]
                + gates[g, 1, 0, blk] * x[1]
                + gates[g, 2, 0, blk] * x[2]
            )


def weigh_kernel(order, sizes, mixed, left, message):
    depth, width = mixed.shape[2:]
    first = place()[0] * depth
    columns = left[...]
    lane = lax.broadcasted_iota(jnp.int32, columns.shape, 1)
    row = lax.broadcasted_iota(jnp.int32, (depth, 1), 0) + first
    bond = lax.broadcasted_iota(jnp.int32, (1, width), 1)
    for d in range(NEAR):
        for j in range(PAIRS):
            blk = order[(d // 2) * NZ + 2 * j + d % 2]
            size = sizes[blk]
            scale = jnp.sum(jnp.where(lane == blk, columns, 0.0), axis=1, keepdims=True)
            scale = jnp.where(row < size, scale, 0.0)
            for g in range(3):
                rows = jnp.where(bond < size, mixed[blk, g] * scale, 0.0)
                message[d, j, g] = rows.astype(jnp.bfloat16)


def contract_kernel(rows_in, sketch, out, exact):
    near, pairs, phys, depth, width = rows_in.shape
    basis = sketch[...]

    def rows_of(j):
        return rows_in[:, j].reshape(near * phys * depth, width)

    samples = [
        lax.dot_general(basis, rows_of(j), OVER_LANES, preferred_element_type=jnp.float32)
        for j in range(pairs)
    ]
    for j in range(pairs):
        projected = jnp.dot(
            samples[j].astype(jnp.bfloat16), rows_of(j), preferred_element_type=jnp.float32
        )
        out[j] = projected.astype(jnp.bfloat16)
        exact[j] = projected


def solve_kernel(order, sizes, ranks, parts, exact, sketch, right_out, norm_out):
    me, _, pair, _ = place()
    pairs, rank, width = parts.shape
    blk = order[me]
    kept = jnp.minimum(ranks[blk], sizes[blk] // 2)

    projected = exact[pair]
    for p in range(pairs):
        projected = projected + jnp.where(pair == p, 0.0, parts[p].astype(jnp.float32))
    prow = lax.broadcasted_iota(jnp.int32, (rank, width), 0)
    projected = jnp.where(prow < kept, projected, 0.0)
    high = projected.astype(jnp.bfloat16)
    rest = projected - high.astype(jnp.float32)
    middle = rest.astype(jnp.bfloat16)
    low = (rest - middle.astype(jnp.float32)).astype(jnp.bfloat16)

    basis = sketch[...]
    fill = jnp.zeros((LANES - rank, width), jnp.bfloat16)
    three = lax.dot_general(
        jnp.concatenate([high, middle, low], axis=0),
        jnp.concatenate([basis, fill], axis=0),
        OVER_LANES,
        preferred_element_type=jnp.float32,
    )
    mirror = lax.dot_general(
        basis,
        jnp.concatenate([high, fill, middle, fill, low, fill], axis=0),
        OVER_LANES,
        preferred_element_type=jnp.float32,
    )
    gram = three[:rank] + three[rank : 2 * rank] + three[2 * rank :]
    mirror = mirror[:, :LANES] + mirror[:, LANES : 2 * LANES] + mirror[:, 2 * LANES :]
    row = lax.broadcasted_iota(jnp.int32, (rank, LANES), 0)
    lane = lax.broadcasted_iota(jnp.int32, (rank, LANES), 1)
    gram = jnp.where((row < kept) & (lane < kept), 0.5 * (gram + mirror), 0.0)
    gram = jnp.where((row == lane) & (row >= kept), 1.0, gram)
    work = jnp.where(lane == row + HALF, 1.0, gram)

    step = 12
    inverse = []
    for k0 in range(0, rank, step):
        height = rank - k0
        heads = [work[j : j + 1, :] for j in range(step)]
        cols = [
            jnp.broadcast_to(work[:, k0 + j : k0 + j + 1], (height, LANES)) for j in range(step)
        ]
        scaled = []
        for j in range(step):
            pivot = cols[j][j : j + 1, :]
            inv = 1.0 / pivot
            scaled.append(heads[j] * inv)
            inverse.append(heads[j] * lax.rsqrt(pivot))
            for i in range(j + 1, step):
                factor = cols[j][i : i + 1, :]
                heads[i] = heads[i] - factor * scaled[j]
                cols[i] = cols[i] - cols[j] * (factor * inv)
        if height > step:
            work = work[step:, :]
            for j in range(step):
                work = work - cols[j][step:, :] * scaled[j]
    lower_inverse = jnp.where(lane >= HALF, jnp.concatenate(inverse, axis=0), 0.0)

    first = lower_inverse.astype(jnp.bfloat16)
    second = (lower_inverse - first.astype(jnp.float32)).astype(jnp.bfloat16)
    above = jnp.zeros((HALF, width), jnp.bfloat16)
    below = jnp.zeros((LANES - HALF - rank, width), jnp.bfloat16)
    right = jnp.dot(
        jnp.concatenate([first, second, first], axis=1),
        jnp.concatenate([above, high, below, above, high, below, above, middle, below], axis=0),
        preferred_element_type=jnp.float32,
    )
    right_out[...] = right
    square = right * right
    folded = square[:, 0:LANES]
    for c in range(LANES, width, LANES):
        folded = folded + square[:, c : c + LANES]
    folded = jnp.sum(folded, axis=0, keepdims=True)
    norm_out[...] = jnp.broadcast_to(folded, norm_out.shape)


def finish_kernel(count, right, norms, out):
    total = jnp.sum(jnp.sum(norms[...], axis=0, keepdims=True), axis=1, keepdims=True)
    out[...] = (right[...] * jnp.sqrt(count / total)).astype(out.dtype)


SMEM = pl.BlockSpec(memory_space=pltpu.SMEM)
VMEM = pl.BlockSpec(memory_space=pltpu.VMEM)


def body(theta, gates, edge_weights, sizes, ranks, order, sketch):
    theta, edge_weights, sketch = theta[0], edge_weights[0], sketch[0]
    sizes, ranks, order = sizes[0], ranks[0], order[0]
    count, phys, depth, width = theta.shape
    rank = sketch.shape[1]
    stretches = lax.axis_size("stretch")
    left = lax.ppermute(
        edge_weights.T, "stretch", [(i, (i + 1) % stretches) for i in range(stretches)]
    )
    mixed = pl.pallas_call(
        mix_kernel,
        out_shape=jax.ShapeDtypeStruct(theta.shape, jnp.float32),
        in_specs=[SMEM, VMEM],
        out_specs=VMEM,
        compiler_params=pltpu.CompilerParams(vmem_limit_bytes=16 * 2**20),
        cost_estimate=pl.CostEstimate(
            flops=15 * theta.size, bytes_accessed=6 * theta.size, transcendentals=0
        ),
        name="mix",
    )(jnp.transpose(gates, (2, 3, 0, 1)), theta)
    message = pl.pallas_call(
        weigh_kernel,
        out_shape=jax.ShapeDtypeStruct((NEAR, PAIRS, phys, depth, width), theta.dtype),
        in_specs=[SMEM, SMEM, VMEM, VMEM],
        out_specs=VMEM,
        compiler_params=pltpu.CompilerParams(vmem_limit_bytes=16 * 2**20),
        name="weigh",
    )(order, sizes, mixed, left)
    rows_in = lax.all_to_all(
        message, "worker", 0, 0, tiled=True, axis_index_groups=NEAR_GROUPS
    )
    parts, exact = pl.pallas_call(
        contract_kernel,
        out_shape=(
            jax.ShapeDtypeStruct((PAIRS, rank, width), jnp.bfloat16),
            jax.ShapeDtypeStruct((PAIRS, rank, width), jnp.float32),
        ),
        in_specs=[VMEM, VMEM],
        out_specs=(VMEM, VMEM),
        compiler_params=pltpu.CompilerParams(vmem_limit_bytes=16 * 2**20),
        name="contract",
    )(rows_in, sketch.T)
    parts = lax.all_to_all(parts, "worker", 0, 0, tiled=True, axis_index_groups=FAR_GROUPS)
    right, norms = pl.pallas_call(
        solve_kernel,
        out_shape=(
            jax.ShapeDtypeStruct((rank, width), jnp.float32),
            jax.ShapeDtypeStruct((WORKERS, LANES), jnp.float32),
        ),
        in_specs=[SMEM, SMEM, SMEM, VMEM, VMEM, VMEM],
        out_specs=(VMEM, VMEM),
        compiler_params=pltpu.CompilerParams(vmem_limit_bytes=16 * 2**20),
        name="solve",
    )(order, sizes, ranks, parts, exact, sketch.T)
    norms = lax.all_to_all(norms, "worker", 0, 0, tiled=True)
    factors = pl.pallas_call(
        functools.partial(finish_kernel, float(count)),
        out_shape=jax.ShapeDtypeStruct((rank, width), jnp.bfloat16),
        in_specs=[VMEM, VMEM],
        out_specs=VMEM,
        compiler_params=pltpu.CompilerParams(vmem_limit_bytes=16 * 2**20),
        name="finish",
    )(right, norms)
    return factors[None, None]


def solution(mesh):
    return jax.shard_map(
        body,
        mesh=mesh,
        in_specs=(
            P("stretch", None, None, "worker", None),
            P("stretch", None, None, None),
            P("stretch", None, "worker"),
            P("stretch", None),
            P("stretch", None),
            P("stretch", None),
            P("stretch", None, None),
        ),
        out_specs=P("stretch", "worker", None, None),
        check_vma=False,
    )
```

```python
import functools

import jax
import jax.numpy as jnp
from jax import lax
from jax.experimental import pallas as pl
from jax.experimental.pallas import tpu as pltpu
from jax.sharding import PartitionSpec as P

NX = 4
NZ = 8
PAIRS = NZ // 2
NEAR = NX * 2
WORKERS = NX * NZ
NEAR_GROUPS = [[x * NZ + 2 * p + q for x in range(NX) for q in range(2)] for p in range(PAIRS)]
FAR_GROUPS = [[x * NZ + 2 * p + q for p in range(PAIRS)] for x in range(NX) for q in range(2)]
LANES = 128
HALF = 64
COST = 100
OVER_LANES = (((1,), (1,)), ((), ()))


def place():
    me = lax.axis_index("worker")
    column, depth = me // NZ, me % NZ
    return me, column, depth // 2, depth % 2


def mix_kernel(gates, theta, mixed):
    for blk in range(theta.shape[0]):
        x = [theta[blk, p].astype(jnp.float32) for p in range(3)]
        for g in range(3):
            mixed[blk, g] = (
                gates[g, 0, 0, blk] * x[0]
                + gates[g, 1, 0, blk] * x[1]
                + gates[g, 2, 0, blk] * x[2]
            )


def weigh_kernel(order, sizes, mixed, left, message):
    depth, width = mixed.shape[2:]
    first = place()[0] * depth
    columns = left[...]
    lane = lax.broadcasted_iota(jnp.int32, columns.shape, 1)
    row = lax.broadcasted_iota(jnp.int32, (depth, 1), 0) + first
    bond = lax.broadcasted_iota(jnp.int32, (1, width), 1)
    for d in range(NEAR):
        for j in range(PAIRS):
            blk = order[(d // 2) * NZ + 2 * j + d % 2]
            size = sizes[blk]
            scale = jnp.sum(jnp.where(lane == blk, columns, 0.0), axis=1, keepdims=True)
            scale = jnp.where(row < size, scale, 0.0)
            for g in range(3):
                rows = jnp.where(bond < size, mixed[blk, g] * scale, 0.0)
                message[d, j, g] = rows.astype(jnp.bfloat16)


def contract_kernel(flip, rows_in, sketch, *refs):
    near, _, phys, depth, width = rows_in.shape
    out = refs[-1]
    rows = rows_in[:, place()[2] ^ flip].reshape(near * phys * depth, width)
    sample = lax.dot_general(
        sketch[...], rows, OVER_LANES, preferred_element_type=jnp.float32
    )
    projected = jnp.dot(sample.astype(jnp.bfloat16), rows, preferred_element_type=jnp.float32)
    out[...] = projected.astype(out.dtype)


def solve_kernel(order, sizes, ranks, exact, part1, part2, part3, sketch, right_out, norm_out):
    me = place()[0]
    rank, width = exact.shape
    blk = order[me]
    kept = jnp.minimum(ranks[blk], sizes[blk] // 2)

    projected = exact[...]
    for part in (part1, part2, part3):
        projected = projected + part[...].astype(jnp.float32)
    prow = lax.broadcasted_iota(jnp.int32, (rank, width), 0)
    projected = jnp.where(prow < kept, projected, 0.0)
    high = projected.astype(jnp.bfloat16)
    rest = projected - high.astype(jnp.float32)
    middle = rest.astype(jnp.bfloat16)
    low = (rest - middle.astype(jnp.float32)).astype(jnp.bfloat16)

    basis = sketch[...]
    fill = jnp.zeros((LANES - rank, width), jnp.bfloat16)
    three = lax.dot_general(
        jnp.concatenate([high, middle, low], axis=0),
        jnp.concatenate([basis, fill], axis=0),
        OVER_LANES,
        preferred_element_type=jnp.float32,
    )
    mirror = lax.dot_general(
        basis,
        jnp.concatenate([high, fill, middle, fill, low, fill], axis=0),
        OVER_LANES,
        preferred_element_type=jnp.float32,
    )
    gram = three[:rank] + three[rank : 2 * rank] + three[2 * rank :]
    mirror = mirror[:, :LANES] + mirror[:, LANES : 2 * LANES] + mirror[:, 2 * LANES :]
    row = lax.broadcasted_iota(jnp.int32, (rank, LANES), 0)
    lane = lax.broadcasted_iota(jnp.int32, (rank, LANES), 1)
    gram = jnp.where((row < kept) & (lane < kept), 0.5 * (gram + mirror), 0.0)
    gram = jnp.where((row == lane) & (row >= kept), 1.0, gram)
    work = jnp.where(lane == row + HALF, 1.0, gram)

    step = 12
    inverse = []
    for k0 in range(0, rank, step):
        height = rank - k0
        heads = [work[j : j + 1, :] for j in range(step)]
        cols = [
            jnp.broadcast_to(work[:, k0 + j : k0 + j + 1], (height, LANES)) for j in range(step)
        ]
        scaled = []
        for j in range(step):
            pivot = cols[j][j : j + 1, :]
            inv = 1.0 / pivot
            scaled.append(heads[j] * inv)
            inverse.append(heads[j] * lax.rsqrt(pivot))
            for i in range(j + 1, step):
                factor = cols[j][i : i + 1, :]
                heads[i] = heads[i] - factor * scaled[j]
                cols[i] = cols[i] - cols[j] * (factor * inv)
        if height > step:
            work = work[step:, :]
            for j in range(step):
                work = work - cols[j][step:, :] * scaled[j]
    lower_inverse = jnp.where(lane >= HALF, jnp.concatenate(inverse, axis=0), 0.0)

    first = lower_inverse.astype(jnp.bfloat16)
    second = (lower_inverse - first.astype(jnp.float32)).astype(jnp.bfloat16)
    above = jnp.zeros((HALF, width), jnp.bfloat16)
    below = jnp.zeros((LANES - HALF - rank, width), jnp.bfloat16)
    right = jnp.dot(
        jnp.concatenate([first, second, first], axis=1),
        jnp.concatenate([above, high, below, above, high, below, above, middle, below], axis=0),
        preferred_element_type=jnp.float32,
    )
    right_out[...] = right
    square = right * right
    folded = square[:, 0:LANES]
    for c in range(LANES, width, LANES):
        folded = folded + square[:, c : c + LANES]
    folded = jnp.sum(folded, axis=0, keepdims=True)
    norm_out[...] = jnp.broadcast_to(folded, norm_out.shape)


def finish_kernel(count, right, norms, out):
    total = jnp.sum(jnp.sum(norms[...], axis=0, keepdims=True), axis=1, keepdims=True)
    out[...] = (right[...] * jnp.sqrt(count / total)).astype(out.dtype)


SMEM = pl.BlockSpec(memory_space=pltpu.SMEM)
VMEM = pl.BlockSpec(memory_space=pltpu.VMEM)


def body(theta, gates, edge_weights, sizes, ranks, order, sketch):
    theta, edge_weights, sketch = theta[0], edge_weights[0], sketch[0]
    sizes, ranks, order = sizes[0], ranks[0], order[0]
    count, phys, depth, width = theta.shape
    rank = sketch.shape[1]
    stretches = lax.axis_size("stretch")
    left = lax.ppermute(
        edge_weights.T, "stretch", [(i, (i + 1) % stretches) for i in range(stretches)]
    )
    mixed = pl.pallas_call(
        mix_kernel,
        out_shape=jax.ShapeDtypeStruct(theta.shape, jnp.float32),
        in_specs=[SMEM, VMEM],
        out_specs=VMEM,
        compiler_params=pltpu.CompilerParams(vmem_limit_bytes=16 * 2**20),
        cost_estimate=pl.CostEstimate(
            flops=15 * theta.size, bytes_accessed=6 * theta.size, transcendentals=0
        ),
        name="mix",
    )(jnp.transpose(gates, (2, 3, 0, 1)), theta)
    message = pl.pallas_call(
        weigh_kernel,
        out_shape=jax.ShapeDtypeStruct((NEAR, PAIRS, phys, depth, width), theta.dtype),
        in_specs=[SMEM, SMEM, VMEM, VMEM],
        out_specs=VMEM,
        compiler_params=pltpu.CompilerParams(vmem_limit_bytes=16 * 2**20),
        name="weigh",
    )(order, sizes, mixed, left)
    rows_in = lax.all_to_all(
        message, "worker", 0, 0, tiled=True, axis_index_groups=NEAR_GROUPS
    )
    parts = {}
    made = ()
    for flip in (2, 3, 1, 0):
        part = pl.pallas_call(
            functools.partial(contract_kernel, flip),
            out_shape=jax.ShapeDtypeStruct((rank, width), jnp.bfloat16 if flip else jnp.float32),
            in_specs=[VMEM, VMEM] + [VMEM] * len(made),
            out_specs=VMEM,
            compiler_params=pltpu.CompilerParams(vmem_limit_bytes=16 * 2**20),
            cost_estimate=pl.CostEstimate(
                flops=COST * rows_in.size, bytes_accessed=COST * rows_in.size, transcendentals=0
            ),
            name=f"contract{flip}",
        )(rows_in, sketch.T, *made)
        made = (part,)
        if flip:
            part = lax.ppermute(part, "worker", [(w, w ^ (2 * flip)) for w in range(WORKERS)])
        parts[flip] = part
    exact = parts[0]
    right, norms = pl.pallas_call(
        solve_kernel,
        out_shape=(
            jax.ShapeDtypeStruct((rank, width), jnp.float32),
            jax.ShapeDtypeStruct((WORKERS, LANES), jnp.float32),
        ),
        in_specs=[SMEM, SMEM, SMEM] + [VMEM] * 5,
        out_specs=(VMEM, VMEM),
        compiler_params=pltpu.CompilerParams(vmem_limit_bytes=16 * 2**20),
        name="solve",
    )(order, sizes, ranks, exact, parts[1], parts[2], parts[3], sketch.T)
    norms = lax.all_to_all(norms, "worker", 0, 0, tiled=True)
    factors = pl.pallas_call(
        functools.partial(finish_kernel, float(count)),
        out_shape=jax.ShapeDtypeStruct((rank, width), jnp.bfloat16),
        in_specs=[VMEM, VMEM],
        out_specs=VMEM,
        compiler_params=pltpu.CompilerParams(vmem_limit_bytes=16 * 2**20),
        name="finish",
    )(right, norms)
    return factors[None, None]


def solution(mesh):
    return jax.shard_map(
        body,
        mesh=mesh,
        in_specs=(
            P("stretch", None, None, "worker", None),
            P("stretch", None, None, None),
            P("stretch", None, "worker"),
            P("stretch", None),
            P("stretch", None),
            P("stretch", None),
            P("stretch", None, None),
        ),
        out_specs=P("stretch", "worker", None, None),
        check_vma=False,
    )
```

```python
import functools

import jax
import jax.numpy as jnp
from jax import lax
from jax.experimental import pallas as pl
from jax.experimental.pallas import tpu as pltpu
from jax.sharding import PartitionSpec as P

NX = 4
NZ = 8
PAIRS = NZ // 2
NEAR = NX * 2
WORKERS = NX * NZ
NEAR_ORDER = [(0, 0), (0, 1), (1, 1), (1, 0), (2, 0), (2, 1), (3, 1), (3, 0)]
NEAR_GROUPS = [[x * NZ + 2 * p + q for x, q in NEAR_ORDER] for p in range(PAIRS)]
FAR_GROUPS = [[x * NZ + 2 * p + q for p in range(PAIRS)] for x in range(NX) for q in range(2)]
LANES = 128
HALF = 64
OVER_LANES = (((1,), (1,)), ((), ()))


def place():
    me = lax.axis_index("worker")
    column, depth = me // NZ, me % NZ
    return me, column, depth // 2, depth % 2


def mix_kernel(gates, theta, mixed):
    for blk in range(theta.shape[0]):
        x = [theta[blk, p].astype(jnp.float32) for p in range(3)]
        for g in range(3):
            mixed[blk, g] = (
                gates[g, 0, 0, blk] * x[0]
                + gates[g, 1, 0, blk] * x[1]
                + gates[g, 2, 0, blk] * x[2]
            )


def weigh_kernel(order, sizes, mixed, left, message):
    depth, width = mixed.shape[2:]
    first = place()[0] * depth
    columns = left[...]
    lane = lax.broadcasted_iota(jnp.int32, columns.shape, 1)
    row = lax.broadcasted_iota(jnp.int32, (depth, 1), 0) + first
    bond = lax.broadcasted_iota(jnp.int32, (1, width), 1)
    for d in range(NEAR):
        for j in range(PAIRS):
            blk = order[NEAR_ORDER[d][0] * NZ + 2 * j + NEAR_ORDER[d][1]]
            size = sizes[blk]
            scale = jnp.sum(jnp.where(lane == blk, columns, 0.0), axis=1, keepdims=True)
            scale = jnp.where(row < size, scale, 0.0)
            for g in range(3):
                rows = jnp.where(bond < size, mixed[blk, g] * scale, 0.0)
                message[d, j, g] = rows.astype(jnp.bfloat16)


def contract_kernel(rows_in, sketch, out, exact):
    near, pairs, phys, depth, width = rows_in.shape
    basis = sketch[...]

    def rows_of(j):
        return rows_in[:, j].reshape(near * phys * depth, width)

    samples = [
        lax.dot_general(basis, rows_of(j), OVER_LANES, preferred_element_type=jnp.float32)
        for j in range(pairs)
    ]
    for j in range(pairs):
        projected = jnp.dot(
            samples[j].astype(jnp.bfloat16), rows_of(j), preferred_element_type=jnp.float32
        )
        out[j] = projected.astype(jnp.bfloat16)
        exact[j] = projected


def solve_kernel(order, sizes, ranks, parts, exact, sketch, right_out, norm_out):
    me, _, pair, _ = place()
    pairs, rank, width = parts.shape
    blk = order[me]
    kept = jnp.minimum(ranks[blk], sizes[blk] // 2)

    projected = exact[pair]
    for p in range(pairs):
        projected = projected + jnp.where(pair == p, 0.0, parts[p].astype(jnp.float32))
    prow = lax.broadcasted_iota(jnp.int32, (rank, width), 0)
    projected = jnp.where(prow < kept, projected, 0.0)
    high = projected.astype(jnp.bfloat16)
    rest = projected - high.astype(jnp.float32)
    middle = rest.astype(jnp.bfloat16)
    low = (rest - middle.astype(jnp.float32)).astype(jnp.bfloat16)

    basis = sketch[...]
    fill = jnp.zeros((LANES - rank, width), jnp.bfloat16)
    three = lax.dot_general(
        jnp.concatenate([high, middle, low], axis=0),
        jnp.concatenate([basis, fill], axis=0),
        OVER_LANES,
        preferred_element_type=jnp.float32,
    )
    mirror = lax.dot_general(
        basis,
        jnp.concatenate([high, fill, middle, fill, low, fill], axis=0),
        OVER_LANES,
        preferred_element_type=jnp.float32,
    )
    gram = three[:rank] + three[rank : 2 * rank] + three[2 * rank :]
    mirror = mirror[:, :LANES] + mirror[:, LANES : 2 * LANES] + mirror[:, 2 * LANES :]
    row = lax.broadcasted_iota(jnp.int32, (rank, LANES), 0)
    lane = lax.broadcasted_iota(jnp.int32, (rank, LANES), 1)
    gram = jnp.where((row < kept) & (lane < kept), 0.5 * (gram + mirror), 0.0)
    gram = jnp.where((row == lane) & (row >= kept), 1.0, gram)
    work = jnp.where(lane == row + HALF, 1.0, gram)

    step = 12
    inverse = []
    for k0 in range(0, rank, step):
        height = rank - k0
        heads = [work[j : j + 1, :] for j in range(step)]
        cols = [
            jnp.broadcast_to(work[:, k0 + j : k0 + j + 1], (height, LANES)) for j in range(step)
        ]
        scaled = []
        for j in range(step):
            pivot = cols[j][j : j + 1, :]
            inv = 1.0 / pivot
            scaled.append(heads[j] * inv)
            inverse.append(heads[j] * lax.rsqrt(pivot))
            for i in range(j + 1, step):
                factor = cols[j][i : i + 1, :]
                heads[i] = heads[i] - factor * scaled[j]
                cols[i] = cols[i] - cols[j] * (factor * inv)
        if height > step:
            work = work[step:, :]
            for j in range(step):
                work = work - cols[j][step:, :] * scaled[j]
    lower_inverse = jnp.where(lane >= HALF, jnp.concatenate(inverse, axis=0), 0.0)

    first = lower_inverse.astype(jnp.bfloat16)
    second = (lower_inverse - first.astype(jnp.float32)).astype(jnp.bfloat16)
    above = jnp.zeros((HALF, width), jnp.bfloat16)
    below = jnp.zeros((LANES - HALF - rank, width), jnp.bfloat16)
    right = jnp.dot(
        jnp.concatenate([first, second, first], axis=1),
        jnp.concatenate([above, high, below, above, high, below, above, middle, below], axis=0),
        preferred_element_type=jnp.float32,
    )
    right_out[...] = right
    square = right * right
    folded = square[:, 0:LANES]
    for c in range(LANES, width, LANES):
        folded = folded + square[:, c : c + LANES]
    folded = jnp.sum(folded, axis=0, keepdims=True)
    norm_out[...] = jnp.broadcast_to(folded, norm_out.shape)


def finish_kernel(count, right, norms, out):
    total = jnp.sum(jnp.sum(norms[...], axis=0, keepdims=True), axis=1, keepdims=True)
    out[...] = (right[...] * jnp.sqrt(count / total)).astype(out.dtype)


SMEM = pl.BlockSpec(memory_space=pltpu.SMEM)
VMEM = pl.BlockSpec(memory_space=pltpu.VMEM)


def body(theta, gates, edge_weights, sizes, ranks, order, sketch):
    theta, edge_weights, sketch = theta[0], edge_weights[0], sketch[0]
    sizes, ranks, order = sizes[0], ranks[0], order[0]
    count, phys, depth, width = theta.shape
    rank = sketch.shape[1]
    stretches = lax.axis_size("stretch")
    left = lax.ppermute(
        edge_weights.T, "stretch", [(i, (i + 1) % stretches) for i in range(stretches)]
    )
    mixed = pl.pallas_call(
        mix_kernel,
        out_shape=jax.ShapeDtypeStruct(theta.shape, jnp.float32),
        in_specs=[SMEM, VMEM],
        out_specs=VMEM,
        compiler_params=pltpu.CompilerParams(vmem_limit_bytes=16 * 2**20),
        cost_estimate=pl.CostEstimate(
            flops=15 * theta.size, bytes_accessed=6 * theta.size, transcendentals=0
        ),
        name="mix",
    )(jnp.transpose(gates, (2, 3, 0, 1)), theta)
    message = pl.pallas_call(
        weigh_kernel,
        out_shape=jax.ShapeDtypeStruct((NEAR, PAIRS, phys, depth, width), theta.dtype),
        in_specs=[SMEM, SMEM, VMEM, VMEM],
        out_specs=VMEM,
        compiler_params=pltpu.CompilerParams(vmem_limit_bytes=16 * 2**20),
        name="weigh",
    )(order, sizes, mixed, left)
    rows_in = lax.all_to_all(
        message, "worker", 0, 0, tiled=True, axis_index_groups=NEAR_GROUPS
    )
    parts, exact = pl.pallas_call(
        contract_kernel,
        out_shape=(
            jax.ShapeDtypeStruct((PAIRS, rank, width), jnp.bfloat16),
            jax.ShapeDtypeStruct((PAIRS, rank, width), jnp.float32),
        ),
        in_specs=[VMEM, VMEM],
        out_specs=(VMEM, VMEM),
        compiler_params=pltpu.CompilerParams(vmem_limit_bytes=16 * 2**20),
        name="contract",
    )(rows_in, sketch.T)
    parts = lax.all_to_all(parts, "worker", 0, 0, tiled=True, axis_index_groups=FAR_GROUPS)
    right, norms = pl.pallas_call(
        solve_kernel,
        out_shape=(
            jax.ShapeDtypeStruct((rank, width), jnp.float32),
            jax.ShapeDtypeStruct((WORKERS, LANES), jnp.float32),
        ),
        in_specs=[SMEM, SMEM, SMEM, VMEM, VMEM, VMEM],
        out_specs=(VMEM, VMEM),
        compiler_params=pltpu.CompilerParams(vmem_limit_bytes=16 * 2**20),
        name="solve",
    )(order, sizes, ranks, parts, exact, sketch.T)
    norms = lax.all_to_all(norms, "worker", 0, 0, tiled=True)
    factors = pl.pallas_call(
        functools.partial(finish_kernel, float(count)),
        out_shape=jax.ShapeDtypeStruct((rank, width), jnp.bfloat16),
        in_specs=[VMEM, VMEM],
        out_specs=VMEM,
        compiler_params=pltpu.CompilerParams(vmem_limit_bytes=16 * 2**20),
        name="finish",
    )(right, norms)
    return factors[None, None]


def solution(mesh):
    return jax.shard_map(
        body,
        mesh=mesh,
        in_specs=(
            P("stretch", None, None, "worker", None),
            P("stretch", None, None, None),
            P("stretch", None, "worker"),
            P("stretch", None),
            P("stretch", None),
            P("stretch", None),
            P("stretch", None, None),
        ),
        out_specs=P("stretch", "worker", None, None),
        check_vma=False,
    )
```

```python
import functools

import jax
import jax.numpy as jnp
from jax import lax
from jax.experimental import pallas as pl
from jax.experimental.pallas import tpu as pltpu
from jax.sharding import PartitionSpec as P

NX = 4
NZ = 8
PAIRS = NZ // 2
NEAR = NX * 2
WORKERS = NX * NZ
NEAR_ORDER = [(0, 0), (0, 1), (1, 1), (1, 0), (2, 0), (2, 1), (3, 1), (3, 0)]
NEAR_GROUPS = [[x * NZ + 2 * p + q for x, q in NEAR_ORDER] for p in range(PAIRS)]
FAR_GROUPS = [[x * NZ + 2 * p + q for p in range(PAIRS)] for x in range(NX) for q in range(2)]
LANES = 128
HALF = 64
OVER_LANES = (((1,), (1,)), ((), ()))


def place():
    me = lax.axis_index("worker")
    column, depth = me // NZ, me % NZ
    return me, column, depth // 2, depth % 2


def mix_kernel(gates, theta, mixed):
    for blk in range(theta.shape[0]):
        x = [theta[blk, p].astype(jnp.float32) for p in range(3)]
        for g in range(3):
            mixed[blk, g] = (
                gates[g, 0, 0, blk] * x[0]
                + gates[g, 1, 0, blk] * x[1]
                + gates[g, 2, 0, blk] * x[2]
            )


def weigh_kernel(order, sizes, mixed, left, message):
    depth, width = mixed.shape[2:]
    first = place()[0] * depth
    columns = left[...]
    lane = lax.broadcasted_iota(jnp.int32, columns.shape, 1)
    row = lax.broadcasted_iota(jnp.int32, (depth, 1), 0) + first
    bond = lax.broadcasted_iota(jnp.int32, (1, width), 1)
    for d in range(NEAR):
        for j in range(PAIRS):
            blk = order[NEAR_ORDER[d][0] * NZ + 2 * j + NEAR_ORDER[d][1]]
            size = sizes[blk]
            scale = jnp.sum(jnp.where(lane == blk, columns, 0.0), axis=1, keepdims=True)
            scale = jnp.where(row < size, scale, 0.0)
            for g in range(3):
                rows = jnp.where(bond < size, mixed[blk, g] * scale, 0.0)
                message[d, j, g] = rows.astype(jnp.bfloat16)


def contract_kernel(rows_in, sketch, out, exact):
    near, pairs, phys, depth, width = rows_in.shape
    basis = sketch[...]

    def rows_of(j):
        return rows_in[:, j].reshape(near * phys * depth, width)

    samples = [
        lax.dot_general(basis, rows_of(j), OVER_LANES, preferred_element_type=jnp.float32)
        for j in range(pairs)
    ]
    for j in range(pairs):
        projected = jnp.dot(
            samples[j].astype(jnp.bfloat16), rows_of(j), preferred_element_type=jnp.float32
        )
        out[j] = projected.astype(jnp.bfloat16)
        exact[j] = projected


def solve_kernel(order, sizes, ranks, parts, exact, sketch, right_out, norm_out):
    me, _, pair, _ = place()
    pairs, rank, width = parts.shape
    blk = order[me]
    kept = jnp.minimum(ranks[blk], sizes[blk] // 2)

    projected = exact[pair]
    for flip in range(1, pairs):
        projected = projected + parts[pair ^ flip].astype(jnp.float32)
    prow = lax.broadcasted_iota(jnp.int32, (rank, width), 0)
    projected = jnp.where(prow < kept, projected, 0.0)
    high = projected.astype(jnp.bfloat16)
    rest = projected - high.astype(jnp.float32)
    middle = rest.astype(jnp.bfloat16)
    low = (rest - middle.astype(jnp.float32)).astype(jnp.bfloat16)

    basis = sketch[...]
    fill = jnp.zeros((LANES - rank, width), jnp.bfloat16)
    three = lax.dot_general(
        jnp.concatenate([high, middle, low], axis=0),
        jnp.concatenate([basis, fill], axis=0),
        OVER_LANES,
        preferred_element_type=jnp.float32,
    )
    mirror = lax.dot_general(
        basis,
        jnp.concatenate([high, fill, middle, fill, low, fill], axis=0),
        OVER_LANES,
        preferred_element_type=jnp.float32,
    )
    gram = three[:rank] + three[rank : 2 * rank] + three[2 * rank :]
    mirror = mirror[:, :LANES] + mirror[:, LANES : 2 * LANES] + mirror[:, 2 * LANES :]
    row = lax.broadcasted_iota(jnp.int32, (rank, LANES), 0)
    lane = lax.broadcasted_iota(jnp.int32, (rank, LANES), 1)
    gram = jnp.where((row < kept) & (lane < kept), 0.5 * (gram + mirror), 0.0)
    gram = jnp.where((row == lane) & (row >= kept), 1.0, gram)
    work = jnp.where(lane == row + HALF, 1.0, gram)

    step = 12
    inverse = []
    for k0 in range(0, rank, step):
        height = rank - k0
        heads = [work[j : j + 1, :] for j in range(step)]
        cols = [
            jnp.broadcast_to(work[:, k0 + j : k0 + j + 1], (height, LANES)) for j in range(step)
        ]
        scaled = []
        for j in range(step):
            pivot = cols[j][j : j + 1, :]
            inv = 1.0 / pivot
            scaled.append(heads[j] * inv)
            inverse.append(heads[j] * lax.rsqrt(pivot))
            for i in range(j + 1, step):
                factor = cols[j][i : i + 1, :]
                heads[i] = heads[i] - factor * scaled[j]
                cols[i] = cols[i] - cols[j] * (factor * inv)
        if height > step:
            work = work[step:, :]
            for j in range(step):
                work = work - cols[j][step:, :] * scaled[j]
    lower_inverse = jnp.where(lane >= HALF, jnp.concatenate(inverse, axis=0), 0.0)

    first = lower_inverse.astype(jnp.bfloat16)
    second = (lower_inverse - first.astype(jnp.float32)).astype(jnp.bfloat16)
    above = jnp.zeros((HALF, width), jnp.bfloat16)
    below = jnp.zeros((LANES - HALF - rank, width), jnp.bfloat16)
    right = jnp.dot(
        jnp.concatenate([first, second, first], axis=1),
        jnp.concatenate([above, high, below, above, high, below, above, middle, below], axis=0),
        preferred_element_type=jnp.float32,
    )
    right_out[...] = right
    square = right * right
    folded = square[:, 0:LANES]
    for c in range(LANES, width, LANES):
        folded = folded + square[:, c : c + LANES]
    folded = jnp.sum(folded, axis=0, keepdims=True)
    norm_out[...] = jnp.broadcast_to(folded, norm_out.shape)


def finish_kernel(count, right, norms, out):
    total = jnp.sum(jnp.sum(norms[...], axis=0, keepdims=True), axis=1, keepdims=True)
    out[...] = (right[...] * jnp.sqrt(count / total)).astype(out.dtype)


SMEM = pl.BlockSpec(memory_space=pltpu.SMEM)
VMEM = pl.BlockSpec(memory_space=pltpu.VMEM)


def body(theta, gates, edge_weights, sizes, ranks, order, sketch):
    theta, edge_weights, sketch = theta[0], edge_weights[0], sketch[0]
    sizes, ranks, order = sizes[0], ranks[0], order[0]
    count, phys, depth, width = theta.shape
    rank = sketch.shape[1]
    stretches = lax.axis_size("stretch")
    left = lax.ppermute(
        edge_weights.T, "stretch", [(i, (i + 1) % stretches) for i in range(stretches)]
    )
    mixed = pl.pallas_call(
        mix_kernel,
        out_shape=jax.ShapeDtypeStruct(theta.shape, jnp.float32),
        in_specs=[SMEM, VMEM],
        out_specs=VMEM,
        compiler_params=pltpu.CompilerParams(vmem_limit_bytes=16 * 2**20),
        cost_estimate=pl.CostEstimate(
            flops=15 * theta.size, bytes_accessed=6 * theta.size, transcendentals=0
        ),
        name="mix",
    )(jnp.transpose(gates, (2, 3, 0, 1)), theta)
    message = pl.pallas_call(
        weigh_kernel,
        out_shape=jax.ShapeDtypeStruct((NEAR, PAIRS, phys, depth, width), theta.dtype),
        in_specs=[SMEM, SMEM, VMEM, VMEM],
        out_specs=VMEM,
        compiler_params=pltpu.CompilerParams(vmem_limit_bytes=16 * 2**20),
        name="weigh",
    )(order, sizes, mixed, left)
    rows_in = lax.all_to_all(
        message, "worker", 0, 0, tiled=True, axis_index_groups=NEAR_GROUPS
    )
    parts, exact = pl.pallas_call(
        contract_kernel,
        out_shape=(
            jax.ShapeDtypeStruct((PAIRS, rank, width), jnp.bfloat16),
            jax.ShapeDtypeStruct((PAIRS, rank, width), jnp.float32),
        ),
        in_specs=[VMEM, VMEM],
        out_specs=(VMEM, VMEM),
        compiler_params=pltpu.CompilerParams(vmem_limit_bytes=16 * 2**20),
        name="contract",
    )(rows_in, sketch.T)
    parts = lax.all_to_all(parts, "worker", 0, 0, tiled=True, axis_index_groups=FAR_GROUPS)
    right, norms = pl.pallas_call(
        solve_kernel,
        out_shape=(
            jax.ShapeDtypeStruct((rank, width), jnp.float32),
            jax.ShapeDtypeStruct((WORKERS, LANES), jnp.float32),
        ),
        in_specs=[SMEM, SMEM, SMEM, VMEM, VMEM, VMEM],
        out_specs=(VMEM, VMEM),
        compiler_params=pltpu.CompilerParams(vmem_limit_bytes=16 * 2**20),
        name="solve",
    )(order, sizes, ranks, parts, exact, sketch.T)
    norms = lax.all_to_all(norms, "worker", 0, 0, tiled=True)
    factors = pl.pallas_call(
        functools.partial(finish_kernel, float(count)),
        out_shape=jax.ShapeDtypeStruct((rank, width), jnp.bfloat16),
        in_specs=[VMEM, VMEM],
        out_specs=VMEM,
        compiler_params=pltpu.CompilerParams(vmem_limit_bytes=16 * 2**20),
        name="finish",
    )(right, norms)
    return factors[None, None]


def solution(mesh):
    return jax.shard_map(
        body,
        mesh=mesh,
        in_specs=(
            P("stretch", None, None, "worker", None),
            P("stretch", None, None, None),
            P("stretch", None, "worker"),
            P("stretch", None),
            P("stretch", None),
            P("stretch", None),
            P("stretch", None, None),
        ),
        out_specs=P("stretch", "worker", None, None),
        check_vma=False,
    )
```
